32 devices in a mesh: phase: 4 (over y, x), tile: 4 (over z), dp: 2 (over core).
Axes of the slice: x: 2, y: 2, z: 4, core: 2. Of those that a mesh axis runs over, the one named last changes fastest.
Arguments:
- camera_feats: bfloat16 [4, 2, 3, 4, 176, 128], P(None, 'dp', None, 'tile'), may hold values from -6 to 6
- backbone_w: bfloat16 [4, 1152, 128], P('phase'), may hold values from -0.1875 to 0.1875
- depth_w: bfloat16 [128, 118], replicated, may hold values from -1 to 1
- block_tile: int32 [4, 2, 1056, 1], P('phase', 'dp', 'tile'), may hold values from 0 to 3; in each aligned block of 264 rows (0 to 263, 264 to 527, ..., all dimensions but the last counted through in order) at most 264 rows name the same one
- point_slot: int32 [4, 2, 1056, 236], P('phase', 'dp', 'tile'), may hold values from 0 to 15
- block_cells: int32 [4, 2, 1056, 16], P('phase', 'dp', 'tile'), may hold values from 0 to 1024, as said below
- bev_w: bfloat16 [1152, 128], replicated, may hold values from -0.1875 to 0.1875
- cotangent: bfloat16 [4, 2, 16, 256, 128], P('phase', 'dp', 'tile'), may hold values from -6 to 6
Outputs:
- encoded: bfloat16 [4, 2, 16, 256, 128], P('phase', 'dp', 'tile')
- conv_grad: float32 [128, 1152], P('tile')
The draws below stay inside these ranges and needn't reach their ends.
Inputs may be any that keep to these rules, and one draw needn't show every extreme that they name: `block_tile`: among the 264 blocks of one sample on one index of tile (an aligned run of rows), at most 264 name the same tile. `block_cells`: 1024 marks a slot whose cell lies outside the grid.
All inputs are finite; a program needn't handle non-finite values.
Results may differ from the reference program's by a relative error of at most 0.0085.
Values may be sent and summed in bfloat16 or wider, within the bound.
A program may use at most 64 MiB of HBM per device.

```python
import math
import jax
import jax.numpy as jnp
import numpy as np
from jax import lax

C = 128
DEPTH = 118
NSEG = 2
DSEG = 59
BLK = 4
POINTS = 236
SLOTS = 16
CAMS = 3
COLS = 176
ROWS_DEV = 1
BEV_COLS = 256
M = 4
BATCH = 2
IMG_ROWS = 4
P_DEV = 528
NBLK = 264
NBLK_ALL = 1056
CAP = 264
BEV_ROWS = 16
CELLS_TILE = 1024
N_PHASE = 4
N_TILE = 4


def draw_block_cells(key, part):
    key = jax.random.fold_in(key, 11)
    anchor_key, offset_key, unused_key = jax.random.split(key, 3)
    extent = (M, BATCH, NBLK_ALL, SLOTS)
    anchor = jax.random.randint(anchor_key, (M, BATCH, NBLK_ALL, 1), 0, CELLS_TILE)
    offsets = jax.random.randint(offset_key, extent, 0, 3 * BEV_COLS)
    cell_ids = (anchor + offsets) % CELLS_TILE
    unused = jax.random.randint(unused_key, extent, 0, 8) == 0
    cell_ids = jnp.where(unused, CELLS_TILE, cell_ids)
    first_block = (jnp.arange(NBLK_ALL) % NBLK == 0).reshape(1, 1, NBLK_ALL)
    last_slot = jnp.where(first_block, CELLS_TILE, cell_ids[:, :, :, SLOTS - 1])
    cell_ids = cell_ids.at[:, :, :, SLOTS - 1].set(last_slot)
    return cell_ids.astype(jnp.int32)


def plant(entries, rng, low, largest):
    shape = entries.shape
    index_at = [jax.random.randint(jax.random.fold_in(rng, axis), (), 0, shape[axis]) for axis in range(len(shape))]
    entries = entries.at[tuple(index_at)].set(low)
    longest = shape.index(max(shape))
    index_at[longest] = (index_at[longest] + 1) % shape[longest]
    return entries.at[tuple(index_at)].set(largest)


def with_spikes(array, own_key, source, target, shards_of, factor):
    owner, partner = [(jnp.arange(array.shape[position]) // (array.shape[position] // shards_of)).reshape([-1 if axis == position else 1 for axis in range(array.ndim)]) for position in (source, target)]
    chosen = jax.random.permutation(own_key, shards_of)[partner]
    strong = (owner == chosen) | (owner == (partner + shards_of // 2) % shards_of)
    return jnp.where(strong, factor * array, array)


def block_levels(stream_key, shape, pieces, low, top_value):
    gain = 1.0
    for dim, blocks in pieces:
        steps = jax.random.uniform(jax.random.fold_in(jax.random.fold_in(stream_key, 6), dim), (blocks,), jnp.float32, low / len(pieces), top_value / len(pieces))
        gain = gain * jnp.repeat(jnp.exp(steps), shape[dim] // blocks).reshape((-1,) + (1,) * (len(shape) - 1 - dim))
    return gain


def shared_out(own_key, own, number, rows, number_of, top, reach, skew):
    sequence = jax.random.permutation(own_key, number_of)
    heavy_load, ordinary = load_shares(number_of, rows * top, reach, skew, True), load_shares(number_of, rows * top, reach, skew, False)
    places = jnp.arange(number_of)

    def named(lengths, turn):
        used = int((lengths > 0).sum())
        fixed = max(1, used // 4)
        moved = fixed + (places - fixed + turn * (used - fixed)) % max(1, number_of - fixed)
        return jnp.zeros((number_of,), jnp.int32).at[sequence[jnp.where(places < fixed, places, moved)]].set(jnp.asarray(lengths, jnp.int32))

    lengths = jnp.where(number % 4 == 0, named(heavy_load, number // 4), named(ordinary, number - number // 4 - 1))
    mixed = jax.random.permutation(jax.random.fold_in(own, 3), number_of)
    source_of, receiver = mixed[0:number_of // 2 * 2:2], mixed[1:number_of // 2 * 2:2]
    margin = jnp.minimum(lengths[source_of] - 1, reach - lengths[receiver]) // 2
    margin = jnp.where((source_of == sequence[0]) | (receiver == sequence[0]) | (lengths[receiver] == 0), 0, jnp.maximum(margin, 0))
    moved = jax.random.randint(jax.random.fold_in(own, 4), (number_of // 2,), 0, 1 << 20) % (margin + 1)
    lengths = lengths.at[source_of].add(-moved).at[receiver].add(moved)
    members = jnp.searchsorted(jnp.cumsum(lengths), jnp.arange(rows * top), side="right").astype(jnp.int32)
    table = members.reshape(top, rows).T
    table = table[jax.random.permutation(jax.random.fold_in(own, 1), rows)]
    turn = jax.random.randint(jax.random.fold_in(own, 2), (rows, 1), 0, top)
    return jnp.take_along_axis(table, (jnp.arange(top)[None, :] + turn) % top, axis=1)


def load_shares(count, total, reach, lean, full):
    weights = [(1 << 20) // math.isqrt(standing ** lean) + 1 for standing in range(1, count + 1)]
    largest = reach if full else min(reach, max(-(-total // count), total * weights[0] // sum(weights)))
    least = 1 if total - largest >= count - 1 else 0
    counts, rest = [largest] + [least] * (count - 1), total - largest - least * (count - 1)
    while rest > 0:
        movable = [i for i in range(1, count) if counts[i] < largest] or [i for i in range(1, count) if counts[i] < reach]
        mass, budget = sum([weights[i] for i in movable]), rest
        for i in movable:
            addition = min(reach - counts[i], max(1, budget * weights[i] // mass), rest)
            counts[i] = counts[i] + addition
            rest = rest - addition
    return np.array(counts)


def bell_draw(stream_key, shape, width, limit, shards=(), dtype=jnp.bfloat16):
    drawn = jax.random.normal(stream_key, shape, jnp.float32) * width
    if len(shards) > 0:
        drawn = block_levels(stream_key, shape, shards, -0.22, 0.18) * drawn
    return jnp.clip(drawn, min=-limit, max=limit).astype(dtype)


def noise_with(stream_key, dims, width, reach, cuts, heavy, held_as=jnp.bfloat16):
    drawn = width * jax.random.normal(stream_key, dims, jnp.float32)
    if cuts:
        drawn = drawn * block_levels(stream_key, dims, cuts, -0.22, 0.18)
    return jnp.clip(with_spikes(drawn, jax.random.fold_in(stream_key, 3), *heavy), -reach, reach).astype(held_as)


def setup_inputs(seed: int = 0) -> dict:
    splits = jax.random.split(jax.random.key(seed), 9)
    camera_feats = bell_draw(splits[0], (M, BATCH, CAMS, IMG_ROWS, COLS, C), 1.0, 6.0, ((1, 2), (3, 4)))
    backbone_w = bell_draw(splits[1], (N_PHASE, 9 * C, C), (9 * C) ** -0.5, 0.1875, ((0, 4),))
    depth_w = bell_draw(splits[2], (C, DEPTH), (C // 4) ** -0.5, 1.0)
    block_tile_keys = jax.random.split(jax.random.fold_in(splits[3], 1), M * BATCH * NBLK_ALL // NBLK)
    block_tile_turns = jax.random.permutation(jax.random.fold_in(splits[3], 3), M * BATCH * NBLK_ALL // NBLK)
    block_tile = jax.vmap(lambda own, number: shared_out(jax.random.fold_in(splits[3], 2), own, number, NBLK, N_TILE, 1, CAP, 2))(block_tile_keys, block_tile_turns).reshape((M, BATCH, NBLK_ALL, 1))
    point_slot = plant(jax.random.randint(splits[4], (M, BATCH, NBLK_ALL, POINTS), 0, SLOTS), jax.random.fold_in(splits[4], 1), 0, SLOTS - 1).astype(jnp.int32)
    block_cells = draw_block_cells(jax.random.fold_in(splits[8], 71), 0)
    bev_w = bell_draw(splits[6], (9 * C, C), (9 * C) ** -0.5, 0.1875)
    cotangent = noise_with(splits[7], (M, BATCH, BEV_ROWS, BEV_COLS, C), 1.0, 6.0, ((0, 4), (1, 2), (2, 4)), (2, 4, 4, 2.0))
    return dict(camera_feats=camera_feats, backbone_w=backbone_w, depth_w=depth_w, block_tile=block_tile, point_slot=point_slot, block_cells=block_cells, bev_w=bev_w, cotangent=cotangent)


BOUND = 8.0


def patches_of(tensor):
    leading = tensor.ndim - 3
    padded = jnp.pad(tensor, [(0, 0)] * leading + [(1, 1), (1, 1), (0, 0)])
    row_count = tensor.shape[-3]
    col_count = tensor.shape[-2]
    shifted = [padded[..., row_off:row_off + row_count, col_off:col_off + col_count, :] for row_off in range(3) for col_off in range(3)]
    stacked = jnp.concatenate(shifted, axis=-1)
    return stacked.reshape(-1, stacked.shape[-1])


def section(images, weight):
    hidden = jnp.dot(patches_of(images), weight, preferred_element_type=jnp.float32).reshape(images.shape)
    return (images.astype(jnp.float32) + jax.nn.silu(hidden)).astype(jnp.bfloat16)


def reference(camera_feats, backbone_w, depth_w, block_tile, point_slot, block_cells, bev_w, cotangent):
    samples = M * BATCH
    grid_cells = BEV_ROWS * BEV_COLS
    groups = N_TILE * P_DEV // BLK

    def one_sample(items):
        images, tile_ids, slot_ids, cell_ids, upstream = items
        feats = images
        for level_idx in range(N_PHASE):
            feats = section(feats, backbone_w[level_idx])
        ordered = feats.reshape(CAMS, N_TILE, ROWS_DEV, COLS, C).transpose(1, 0, 2, 3, 4).reshape(N_TILE * P_DEV, C)
        logits = jnp.dot(ordered, depth_w, preferred_element_type=jnp.float32)
        depth_prob = jax.nn.softmax(BOUND * jnp.tanh(logits / BOUND), axis=-1)
        depth_blocks = depth_prob.reshape(groups, BLK, NSEG, DSEG).transpose(0, 2, 1, 3).reshape(NBLK_ALL, BLK, DSEG)
        slot_blocks = slot_ids.reshape(NBLK_ALL, BLK, DSEG)
        splat_w = jnp.stack([jnp.sum(jnp.where(slot_blocks == target, depth_blocks, jnp.zeros_like(depth_blocks)), axis=-1) for target in range(SLOTS)], axis=1).astype(jnp.bfloat16)
        context = jnp.repeat(ordered.reshape(groups, BLK, C), NSEG, axis=0)
        pooled = jnp.einsum("nsb,nbc->nsc", splat_w.astype(jnp.float32), context.astype(jnp.float32)).astype(jnp.bfloat16)
        cell_index = jnp.where(cell_ids == CELLS_TILE, grid_cells, tile_ids.reshape(NBLK_ALL, 1) * CELLS_TILE + cell_ids).astype(jnp.int32)
        totals = jax.ops.segment_sum(pooled.reshape(-1, C).astype(jnp.float32), cell_index.reshape(-1), num_segments=grid_cells + 1)
        bev_grid = totals[:grid_cells].astype(jnp.bfloat16).reshape(BEV_ROWS, BEV_COLS, C)
        bev_patches = patches_of(bev_grid)
        mixed = jnp.dot(bev_patches, bev_w, preferred_element_type=jnp.float32)
        encoded = (bev_grid.astype(jnp.float32).reshape(-1, C) + mixed).astype(jnp.bfloat16).reshape(BEV_ROWS, BEV_COLS, C)
        term = jnp.dot(upstream.reshape(-1, C).T, bev_patches, preferred_element_type=jnp.float32)
        return encoded, term

    items = (
        camera_feats.reshape(samples, CAMS, IMG_ROWS, COLS, C),
        block_tile.reshape(samples, NBLK_ALL),
        point_slot.reshape(samples, NBLK_ALL, POINTS),
        block_cells.reshape(samples, NBLK_ALL, SLOTS),
        cotangent.reshape(samples, BEV_ROWS, BEV_COLS, C),
    )
    encoded_all, terms = lax.map(one_sample, items)
    conv_grad = jnp.sum(terms, axis=0) * (samples * grid_cells) ** -0.5
    return encoded_all.reshape(M, BATCH, BEV_ROWS, BEV_COLS, C), conv_grad
```

```python
import functools

import jax
import jax.numpy as jnp
from jax import lax
from jax.experimental import pallas as pl
from jax.experimental.pallas import tpu as pltpu
from jax.sharding import PartitionSpec as P

NSEG = 2
BLK = 4


BOUND = 8.0


def extended(cells, sides, width):
    for axis, dim in sides:
        count = lax.axis_size(axis)
        ends = count - 1
        head = lax.slice_in_dim(cells, 0, width, axis=dim)
        tail = lax.slice_in_dim(cells, cells.shape[dim] - width, cells.shape[dim], axis=dim)
        cells = jnp.concatenate(
            [
                lax.ppermute(tail, axis, [(i, (i + 1) % count) for i in range(ends)]),
                cells,
                lax.ppermute(head, axis, [((i + 1) % count, i) for i in range(ends)]),
            ],
            axis=dim,
        )
    return cells


def passed_along(block, axis, distance):
    devices = range(lax.axis_size(axis))
    route = [(i - distance, i) for i in devices if i - distance in devices]
    return lax.ppermute(block, axis, route)


def from_root(block, axis, source):
    block = jnp.where(lax.axis_index(axis) == source, block, jnp.zeros_like(block))
    return lax.psum(block, axis)


def patches_from(padded, row_count, col_count):
    widened = jnp.pad(padded, [(0, 0)] * (padded.ndim - 2) + [(1, 1), (0, 0)])
    shifted = [
        widened[..., row_off : row_off + row_count, col_off : col_off + col_count, :]
        for row_off in range(3)
        for col_off in range(3)
    ]
    stacked = jnp.concatenate(shifted, axis=-1)
    return stacked.reshape(-1, stacked.shape[-1])


def section(images, weight):
    padded = extended(images, (("tile", 2),), 1)
    hidden = jnp.dot(
        patches_from(padded, images.shape[2], images.shape[3]),
        weight,
        preferred_element_type=jnp.float32,
    ).reshape(images.shape)
    return (images.astype(jnp.float32) + jax.nn.silu(hidden)).astype(jnp.bfloat16)


def body(camera_feats, backbone_w, depth_w, block_tile, point_slot, block_cells, bev_w, cotangent):
    phases = lax.axis_size("phase")
    phase_idx = lax.axis_index("phase")
    tile_count = lax.axis_size("tile")
    micro_all = camera_feats.shape[0]
    per_phase = micro_all // phases
    own_weight = backbone_w[0]
    carried = jnp.zeros_like(camera_feats[0])
    collected = jnp.zeros_like(camera_feats)
    steps_total = micro_all + phases - 1
    for step_idx in range(steps_total):
        if step_idx < micro_all:
            entering = jnp.where(phase_idx == 0, camera_feats[step_idx], carried)
        else:
            entering = carried
        leaving = section(entering, own_weight)
        finished = step_idx - (phases - 1)
        if finished >= 0:
            collected = collected.at[finished].set(
                jnp.where(phase_idx == phases - 1, leaving, collected[finished])
            )
        if step_idx + 1 < steps_total:
            carried = passed_along(leaving, "phase", 1)
    everything = from_root(collected, "phase", phases - 1)
    own_feats = lax.dynamic_slice_in_dim(everything, phase_idx * per_phase, per_phase, 0)
    samples_dev = own_feats.shape[0] * own_feats.shape[1]
    channels = own_feats.shape[-1]
    context = own_feats.reshape(samples_dev, -1, channels)
    positions = context.shape[1]
    seg_len = depth_w.shape[1] // NSEG
    slot_total = block_cells.shape[-1]
    pos_groups = positions // BLK
    block_count = pos_groups * NSEG
    logits = jnp.dot(context.reshape(-1, channels), depth_w, preferred_element_type=jnp.float32)
    depth_prob = jax.nn.softmax(BOUND * jnp.tanh(logits / BOUND), axis=-1)
    depth_blocks = (
        depth_prob.reshape(samples_dev, pos_groups, BLK, NSEG, seg_len)
        .transpose(0, 1, 3, 2, 4)
        .reshape(samples_dev, block_count, BLK, seg_len)
    )
    slot_blocks = point_slot.reshape(samples_dev, block_count, BLK, seg_len)
    splat_w = jnp.stack(
        [
            jnp.sum(
                jnp.where(slot_blocks == target, depth_blocks, jnp.zeros_like(depth_blocks)),
                axis=-1,
            )
            for target in range(slot_total)
        ],
        axis=2,
    ).astype(jnp.bfloat16)
    block_ctx = jnp.repeat(context.reshape(samples_dev, pos_groups, BLK, channels), NSEG, axis=1)
    row_count = cotangent.shape[2]
    col_count = cotangent.shape[3]
    cells_tile = row_count * col_count
    capacity = max(2, 4 * block_count // tile_count)
    targets = block_tile.reshape(samples_dev, block_count)
    member = (targets[..., None] == jnp.arange(tile_count, dtype=jnp.int32)).astype(jnp.int32)
    slot_rank = jnp.sum((jnp.cumsum(member, axis=1) - 1) * member, axis=-1)
    slot_flat = targets * capacity + slot_rank
    sample_rows = jnp.broadcast_to(
        jnp.arange(samples_dev, dtype=jnp.int32)[:, None], slot_flat.shape
    )
    send_ctx = (
        jnp.zeros((samples_dev, tile_count * capacity, BLK, channels), jnp.bfloat16)
        .at[sample_rows, slot_flat]
        .set(block_ctx)
    )
    send_weights = (
        jnp.zeros((samples_dev, tile_count * capacity, slot_total, BLK), jnp.bfloat16)
        .at[sample_rows, slot_flat]
        .set(splat_w)
    )
    send_cells = (
        jnp.full((samples_dev, tile_count * capacity, slot_total), cells_tile, jnp.int32)
        .at[sample_rows, slot_flat]
        .set(block_cells.reshape(samples_dev, block_count, slot_total))
    )
    send_ctx = send_ctx.reshape(samples_dev, tile_count, capacity, BLK, channels)
    send_weights = send_weights.reshape(samples_dev, tile_count, capacity, slot_total, BLK)
    send_cells = send_cells.reshape(samples_dev, tile_count, capacity, slot_total)
    got_ctx, got_weights, got_cells = (
        lax.all_to_all(send_ctx, "tile", split_axis=1, concat_axis=1, tiled=True),
        lax.all_to_all(send_weights, "tile", split_axis=1, concat_axis=1, tiled=True),
        lax.all_to_all(send_cells, "tile", split_axis=1, concat_axis=1, tiled=True),
    )
    pooled = jnp.einsum(
        "ankti,ankic->anktc", got_weights, got_ctx, preferred_element_type=jnp.float32
    ).astype(jnp.bfloat16)
    group_size = min(8, tile_count)
    group_count = tile_count // group_size
    group_rows = group_size * capacity * slot_total
    pooled_groups = jnp.moveaxis(
        pooled.reshape(samples_dev, group_count, group_rows, channels), 1, 0
    )
    cell_groups = jnp.moveaxis(got_cells.reshape(samples_dev, group_count, group_rows), 1, 0)
    cell_range = jnp.arange(cells_tile, dtype=jnp.int32).reshape(1, cells_tile, 1)

    def splat_group(grid_sum, pieces):
        part_pooled, part_cells = pieces
        one_hot = (part_cells[:, None, :] == cell_range).astype(jnp.bfloat16)
        grid_sum = grid_sum + jnp.einsum(
            "sxr,src->sxc", one_hot, part_pooled, preferred_element_type=jnp.float32
        )
        return (grid_sum, None)

    totals, _ = lax.scan(
        splat_group,
        jnp.zeros((samples_dev, cells_tile, channels), jnp.float32),
        (pooled_groups, cell_groups),
    )
    bev_grid = totals.astype(jnp.bfloat16).reshape(samples_dev, row_count, col_count, channels)
    padded_grid = extended(bev_grid, (("tile", 1),), 1)
    bev_patches = patches_from(padded_grid, row_count, col_count)
    mixed = jnp.dot(bev_patches, bev_w, preferred_element_type=jnp.float32)
    encoded = (
        (bev_grid.astype(jnp.float32).reshape(-1, channels) + mixed)
        .astype(jnp.bfloat16)
        .reshape(cotangent.shape)
    )
    upstream = cotangent.reshape(-1, channels)
    total_cells = (
        micro_all * cotangent.shape[1] * lax.axis_size("dp") * row_count * tile_count * col_count
    )
    grad_scale = float(total_cells) ** (-0.5)
    grad_share = lax.psum_scatter(
        grad_scale
        * lax.dot_general(
            upstream, bev_patches, (((0,), (0,)), ((), ())), preferred_element_type=jnp.float32
        ),
        "tile",
        scatter_dimension=0,
        tiled=True,
    )
    conv_grad = lax.psum(grad_share, ("phase", "dp"))
    return (encoded, conv_grad)


MESH = pl.DeviceIdType.MESH
NT = (((1,), (1,)), ((), ()))
TN = (((0,), (0,)), ((), ()))
F32 = jnp.float32
BF16 = jnp.bfloat16


def with_side_columns(block, width):
    rows = block.shape[0]
    wide = block.astype(F32)
    col = lax.broadcasted_iota(jnp.int32, block.shape, 0) % width
    before = jnp.where(col == 0, 0.0, pltpu.roll(wide, 1, 0))
    after = jnp.where(col == width - 1, 0.0, pltpu.roll(wide, rows - 1, 0))
    return before.astype(BF16), block, after.astype(BF16)


def fused_kernel(
    dims,
    cam_ref, w_ref, dw_ref, slots_ref, code_ref, bw_ref, cot_ref,
    enc_ref, grad_ref,
    x_ref, z_ref, wall_ref, codes_ref, acc_w, wt_ref, wr_ref, acc_ref, zb_ref,
    gpart, gsend, grecv_a, gsum, gsend_b, grecv_b, grecv_c, gfin, gfin_other,
    local_sem, row_send, row_recv, code_send, code_recv, w_send, w_recv, f_send, f_recv,
    wt_send, wt_recv, a_send, a_recv, b_send, b_recv, c_send, c_recv, d_send, d_recv,
):
    phases, tiles, width, slots, bins, seg, grid_rows, grid_cols, scale = dims
    ph, ti, dp = lax.axis_index("phase"), lax.axis_index("tile"), lax.axis_index("dp")
    other = 1 - dp
    pos = cam_ref.shape[1]
    channels = cam_ref.shape[2]
    lanes = code_ref.shape[1]
    half = w_ref.shape[0] // 2
    cols3 = 3 * channels

    def tile_peer(k):
        return (ph, lax.rem(ti + k, tiles), dp)

    def phase_peer(k):
        return (lax.rem(ph + k, phases), ti, dp)

    partner = (ph, ti, other)

    barrier = pltpu.get_barrier_semaphore()
    for k in range(1, tiles):
        pl.semaphore_signal(barrier, inc=1, device_id=tile_peer(k), device_id_type=MESH)
    for k in range(1, phases):
        pl.semaphore_signal(barrier, inc=1, device_id=phase_peer(k), device_id_type=MESH)
    pl.semaphore_signal(barrier, inc=1, device_id=partner, device_id_type=MESH)
    pl.semaphore_wait(barrier, tiles - 1 + phases - 1 + 1)

    def remote(src, dst, send, recv, device):
        copy = pltpu.make_async_remote_copy(
            src_ref=src, dst_ref=dst, send_sem=send, recv_sem=recv,
            device_id=device, device_id_type=MESH,
        )
        copy.start()
        return copy

    own_rows = pl.ds(pl.multiple_of(ti * pos, 16), pos)
    own_lanes = pl.ds(pl.multiple_of(ti * lanes, 128), lanes)
    own_half = pl.ds(pl.multiple_of(dp * half, 16), half)
    w_copies = [
        remote(w_ref.at[own_half], wall_ref.at[ph, own_half], w_send.at[k], w_recv.at[k], phase_peer(k))
        for k in range(1, phases)
    ]
    row_copies = [
        remote(cam_ref.at[ph], x_ref.at[own_rows], row_send.at[k], row_recv.at[k], tile_peer(k))
        for k in range(1, tiles)
    ]
    code_copies = [
        remote(code_ref, codes_ref.at[:, own_lanes], code_send.at[k], code_recv.at[k], tile_peer(k))
        for k in range(1, tiles)
    ]
    own = [
        pltpu.make_async_copy(cam_ref.at[ph], x_ref.at[own_rows], local_sem.at[0]),
        pltpu.make_async_copy(code_ref, codes_ref.at[:, own_lanes], local_sem.at[1]),
        pltpu.make_async_copy(w_ref, wall_ref.at[ph], local_sem.at[2]),
    ]
    for copy in own:
        copy.start()

    edge = jnp.zeros((pos, cols3), BF16)
    z_ref[pl.ds(0, pos), :] = edge
    z_ref[pl.ds((tiles + 1) * pos, pos), :] = edge
    acc_ref[...] = jnp.zeros_like(acc_ref)
    acc_w[...] = jnp.zeros_like(acc_w)

    forwards = []
    for k in range(1, phases):
        w_copies[k - 1].wait_recv()
        source = lax.rem(ph - k + phases, phases)
        forwards.append(
            remote(wall_ref.at[source, own_half], wall_ref.at[source, own_half],
                   f_send.at[k], f_recv.at[k], partner)
        )
    for copy in own + row_copies + code_copies + forwards:
        copy.wait()
    for copy in w_copies:
        copy.wait_send()

    @pl.loop(0, phases)
    def _(s):
        @pl.loop(0, tiles)
        def _(u):
            rows = x_ref[pl.ds(pl.multiple_of(u * pos, 16), pos), :]
            at = pl.ds(pl.multiple_of((u + 1) * pos, 16), pos)
            for e, part in enumerate(with_side_columns(rows, width)):
                z_ref[at, e * channels : (e + 1) * channels] = part

        @pl.loop(0, tiles)
        def _(u):
            at = pl.ds(pl.multiple_of(u * pos, 16), pos)
            hidden = jnp.zeros((pos, channels), F32)
            for a in range(3):
                hidden += jnp.dot(
                    z_ref[pl.ds(pl.multiple_of((u + a) * pos, 16), pos), :],
                    wall_ref[s, a * cols3 : (a + 1) * cols3, :],
                    preferred_element_type=F32,
                )
            x_ref[at, :] = (x_ref[at, :].astype(F32) + hidden * jax.nn.sigmoid(hidden)).astype(BF16)

    logits = jnp.dot(x_ref[own_rows, :], dw_ref[...], preferred_element_type=F32)
    lane = lax.broadcasted_iota(jnp.int32, logits.shape, 1)
    inside = (lane % 128) < seg
    raised = jnp.where(inside, jnp.exp(BOUND * jnp.tanh(logits / BOUND)), 0.0)
    prob = raised / jnp.sum(raised, axis=1, keepdims=True)
    half_of = lax.broadcasted_iota(jnp.int32, (bins, 128), 0) // 128
    target_col = lax.broadcasted_iota(jnp.int32, (bins, 128), 1)
    summed = jnp.zeros((pos, 128), F32)
    for t in range(slots):
        chosen = jnp.where(slots_ref[...] == t, prob, 0.0).astype(BF16)
        into = jnp.where(target_col == half_of * slots + t, 1.0, 0.0).astype(BF16)
        summed += jnp.dot(chosen, into, preferred_element_type=F32)
    acc_w[pl.ds(0, pos), :] = summed.astype(BF16)
    names = NSEG * slots
    pick = jnp.where(
        lax.broadcasted_iota(jnp.int32, (names, 128), 0) == lax.broadcasted_iota(jnp.int32, (names, 128), 1),
        1.0, 0.0,
    ).astype(BF16)
    wt_ref[ti] = lax.dot_general(pick, acc_w[...], NT, preferred_element_type=F32).astype(BF16)
    wt_copies = [
        remote(wt_ref.at[ti], wt_ref.at[ti], wt_send.at[k], wt_recv.at[k], tile_peer(k))
        for k in range(1, tiles)
    ]
    for copy in wt_copies:
        copy.wait()

    chunk = 16
    chunk_rows = chunk * names
    chunk_pos = chunk * BLK
    spread = jnp.where(
        lax.broadcasted_iota(jnp.int32, (names, chunk_rows), 1) % names
        == lax.broadcasted_iota(jnp.int32, (names, chunk_rows), 0),
        1.0, 0.0,
    ).astype(BF16)

    @pl.loop(0, tiles)
    def _(u):
        back = wt_ref[u].astype(F32).T.astype(BF16)
        tiled = jnp.dot(back[:pos], spread, preferred_element_type=F32)
        wr_ref[pl.ds(pl.multiple_of(u * pos, 16), pos), :] = tiled.astype(BF16)

    shape = (chunk_pos, chunk_rows)
    same = jnp.where(
        lax.broadcasted_iota(jnp.int32, shape, 0) // BLK == lax.broadcasted_iota(jnp.int32, shape, 1) // names,
        1.0, 0.0,
    ).astype(BF16)
    window = grid_rows + 2

    @pl.loop(0, tiles * pos // chunk_pos)
    def _(c):
        at = pl.ds(pl.multiple_of(c * chunk_pos, 16), chunk_pos)
        weights = wr_ref[at, :] * same
        pooled = lax.dot_general(x_ref[at, :], weights, TN, preferred_element_type=F32).astype(BF16)
        cell = codes_ref[:, pl.ds(pl.multiple_of(c * chunk_rows, 128), chunk_rows)]
        cell = cell - (ti * grid_rows - 1) * grid_cols
        row = cell >> 8
        column = cell & (grid_cols - 1)
        marks = jnp.where(
            lax.broadcasted_iota(jnp.int32, (grid_cols, chunk_rows), 0) == column, 1.0, 0.0
        ).astype(BF16)
        parts = [pooled * jnp.where(row == y, 1.0, 0.0).astype(BF16) for y in range(window)]
        acc_ref[...] += lax.dot_general(
            jnp.concatenate(parts, axis=0), marks, NT, preferred_element_type=F32
        )

    for y in range(window):
        line = acc_ref[y * channels : (y + 1) * channels, :].T.astype(BF16)
        for e, part in enumerate(with_side_columns(line, grid_cols)):
            zb_ref[y * grid_cols : (y + 1) * grid_cols, e * channels : (e + 1) * channels] = part

    cells = grid_rows * grid_cols
    upstream = cot_ref[...].astype(F32).T.astype(BF16)
    for a in range(3):
        term = scale * jnp.dot(
            upstream, zb_ref[a * grid_cols : a * grid_cols + cells, :], preferred_element_type=F32
        )
        for t in range(tiles):
            for d in range(2):
                piece = term[(2 * t + d) * 16 : (2 * t + d + 1) * 16]
                gpart[d, t, :, a * cols3 : (a + 1) * cols3] = piece
                gsend[d, t, :, a * cols3 : (a + 1) * cols3] = piece.astype(BF16)
    to_partner = remote(gsend.at[other], grecv_a, a_send, a_recv, partner)

    for y in range(grid_rows):
        mixed = zb_ref[(y + 1) * grid_cols : (y + 2) * grid_cols, channels : 2 * channels].astype(F32)
        for a in range(3):
            mixed += jnp.dot(
                zb_ref[(y + a) * grid_cols : (y + a + 1) * grid_cols, :],
                bw_ref[a * cols3 : (a + 1) * cols3, :],
                preferred_element_type=F32,
            )
        enc_ref[y * grid_cols : (y + 1) * grid_cols, :] = mixed.astype(BF16)

    to_partner.wait()
    for t in range(tiles):
        total = gpart[dp, t] + grecv_a[t].astype(F32)
        gsum[t] = total
        gsend_b[t] = total.astype(BF16)
    b_copies = [
        remote(gsend_b.at[lax.rem(ti + k, tiles)], grecv_b.at[ti], b_send.at[k], b_recv.at[k], tile_peer(k))
        for k in range(1, tiles)
    ]
    for copy in b_copies:
        copy.wait()
    total = gsum[ti]
    for k in range(1, tiles):
        total += grecv_b[lax.rem(ti + k, tiles)].astype(F32)
    grecv_c[ph] = total.astype(BF16)
    c_copies = [
        remote(grecv_c.at[ph], grecv_c.at[ph], c_send.at[k], c_recv.at[k], phase_peer(k))
        for k in range(1, phases)
    ]
    for copy in c_copies:
        copy.wait()
    total = grecv_c[0].astype(F32)
    for p in range(1, phases):
        total += grecv_c[p].astype(F32)
    gfin[...] = total
    last = remote(gfin, gfin_other, d_send, d_recv, partner)
    grad_ref[dp] = total
    last.wait()
    grad_ref[other] = gfin_other[...]


def fused_body(camera_feats, backbone_w, depth_w, block_tile, point_slot, block_cells, bev_w, cotangent):
    phases, tiles = lax.axis_size("phase"), lax.axis_size("tile")
    micro, _, cams, _, width, channels = camera_feats.shape
    pos = cams * width
    groups = pos // BLK
    seg = depth_w.shape[1] // NSEG
    slots = block_cells.shape[-1]
    grid_rows, grid_cols = cotangent.shape[2:4]
    cells = grid_rows * grid_cols
    side = [(0, 0), (0, 0), (0, 128 - seg)]
    bins = NSEG * 128
    heads = jnp.pad(depth_w.reshape(channels, NSEG, seg), side).reshape(channels, bins)
    point = point_slot.reshape(groups, NSEG, BLK, seg).transpose(0, 2, 1, 3).reshape(pos, NSEG, seg)
    point = jnp.pad(point, side).reshape(pos, bins)
    local = block_cells.reshape(groups * NSEG, slots)
    code = block_tile.reshape(groups * NSEG, 1) * cells + local
    code = jnp.where(local < cells, code, 1 << 24).reshape(1, groups * NSEG * slots)
    total = micro * cotangent.shape[1] * lax.axis_size("dp") * cells * tiles
    dims = (phases, tiles, width, slots, bins, seg, grid_rows, grid_cols, float(total) ** (-0.5))
    rows = code.shape[1]
    cols = 9 * channels
    pad_pos = -(-pos // 128) * 128
    dma = pltpu.SemaphoreType.DMA
    vmem = pl.BlockSpec(memory_space=pltpu.VMEM)
    scratch = [
        pltpu.VMEM((tiles * pos, channels), BF16),
        pltpu.VMEM(((tiles + 2) * pos, 3 * channels), BF16),
        pltpu.VMEM((phases, cols, channels), BF16),
        pltpu.VMEM((1, tiles * rows), jnp.int32),
        pltpu.VMEM((pad_pos, 128), BF16),
        pltpu.VMEM((tiles, NSEG * slots, pad_pos), BF16),
        pltpu.VMEM((tiles * pos, 16 * NSEG * slots), BF16),
        pltpu.VMEM(((grid_rows + 2) * channels, grid_cols), F32),
        pltpu.VMEM(((grid_rows + 2) * grid_cols, 3 * channels), BF16),
        pltpu.VMEM((2, tiles, 16, cols), F32),
        pltpu.VMEM((2, tiles, 16, cols), BF16),
        pltpu.VMEM((tiles, 16, cols), BF16),
        pltpu.VMEM((tiles, 16, cols), F32),
        pltpu.VMEM((tiles, 16, cols), BF16),
        pltpu.VMEM((tiles, 16, cols), BF16),
        pltpu.VMEM((phases, 16, cols), BF16),
        pltpu.VMEM((16, cols), F32),
        pltpu.VMEM((16, cols), F32),
        dma((3,)),
        dma((tiles,)), dma((tiles,)), dma((tiles,)), dma((tiles,)),
        dma((phases,)), dma((phases,)), dma((phases,)), dma((phases,)),
        dma((tiles,)), dma((tiles,)),
        dma(()), dma(()),
        dma((tiles,)), dma((tiles,)),
        dma((phases,)), dma((phases,)),
        dma(()), dma(()),
    ]
    encoded, grad = pl.pallas_call(
        functools.partial(fused_kernel, dims),
        out_shape=(
            jax.ShapeDtypeStruct((cells, channels), BF16),
            jax.ShapeDtypeStruct((2, 16, cols), F32),
        ),
        in_specs=[vmem] * 7,
        out_specs=(vmem, vmem),
        scratch_shapes=scratch,
        compiler_params=pltpu.CompilerParams(
            collective_id=0, has_side_effects=True, vmem_limit_bytes=48 * 1024 * 1024
        ),
        name="lift_splat",
    )(
        camera_feats.reshape(micro, pos, channels),
        backbone_w[0],
        heads,
        point,
        code,
        bev_w,
        cotangent.reshape(cells, channels),
    )
    return encoded.reshape(cotangent.shape), grad.reshape(32, cols)


def solution(mesh):
    return jax.shard_map(
        fused_body if mesh.shape["tile"] == 4 else body,
        mesh=mesh,
        in_specs=(
            P(None, "dp", None, "tile", None, None),
            P("phase", None, None),
            P(),
            P("phase", "dp", "tile", None),
            P("phase", "dp", "tile", None),
            P("phase", "dp", "tile", None),
            P(),
            P("phase", "dp", "tile", None, None),
        ),
        out_specs=(P("phase", "dp", "tile", None, None), P("tile", None)),
        check_vma=False,
    )
```

```python
import functools

import jax
import jax.numpy as jnp
from jax import lax
from jax.experimental import pallas as pl
from jax.experimental.pallas import tpu as pltpu
from jax.sharding import PartitionSpec as P

NSEG = 2
BLK = 4


BOUND = 8.0


def extended(cells, sides, width):
    for axis, dim in sides:
        count = lax.axis_size(axis)
        ends = count - 1
        head = lax.slice_in_dim(cells, 0, width, axis=dim)
        tail = lax.slice_in_dim(cells, cells.shape[dim] - width, cells.shape[dim], axis=dim)
        cells = jnp.concatenate(
            [
                lax.ppermute(tail, axis, [(i, (i + 1) % count) for i in range(ends)]),
                cells,
                lax.ppermute(head, axis, [((i + 1) % count, i) for i in range(ends)]),
            ],
            axis=dim,
        )
    return cells


def passed_along(block, axis, distance):
    devices = range(lax.axis_size(axis))
    route = [(i - distance, i) for i in devices if i - distance in devices]
    return lax.ppermute(block, axis, route)


def from_root(block, axis, source):
    block = jnp.where(lax.axis_index(axis) == source, block, jnp.zeros_like(block))
    return lax.psum(block, axis)


def patches_from(padded, row_count, col_count):
    widened = jnp.pad(padded, [(0, 0)] * (padded.ndim - 2) + [(1, 1), (0, 0)])
    shifted = [
        widened[..., row_off : row_off + row_count, col_off : col_off + col_count, :]
        for row_off in range(3)
        for col_off in range(3)
    ]
    stacked = jnp.concatenate(shifted, axis=-1)
    return stacked.reshape(-1, stacked.shape[-1])


def section(images, weight):
    padded = extended(images, (("tile", 2),), 1)
    hidden = jnp.dot(
        patches_from(padded, images.shape[2], images.shape[3]),
        weight,
        preferred_element_type=jnp.float32,
    ).reshape(images.shape)
    return (images.astype(jnp.float32) + jax.nn.silu(hidden)).astype(jnp.bfloat16)


def body(camera_feats, backbone_w, depth_w, block_tile, point_slot, block_cells, bev_w, cotangent):
    phases = lax.axis_size("phase")
    phase_idx = lax.axis_index("phase")
    tile_count = lax.axis_size("tile")
    micro_all = camera_feats.shape[0]
    per_phase = micro_all // phases
    own_weight = backbone_w[0]
    carried = jnp.zeros_like(camera_feats[0])
    collected = jnp.zeros_like(camera_feats)
    steps_total = micro_all + phases - 1
    for step_idx in range(steps_total):
        if step_idx < micro_all:
            entering = jnp.where(phase_idx == 0, camera_feats[step_idx], carried)
        else:
            entering = carried
        leaving = section(entering, own_weight)
        finished = step_idx - (phases - 1)
        if finished >= 0:
            collected = collected.at[finished].set(
                jnp.where(phase_idx == phases - 1, leaving, collected[finished])
            )
        if step_idx + 1 < steps_total:
            carried = passed_along(leaving, "phase", 1)
    everything = from_root(collected, "phase", phases - 1)
    own_feats = lax.dynamic_slice_in_dim(everything, phase_idx * per_phase, per_phase, 0)
    samples_dev = own_feats.shape[0] * own_feats.shape[1]
    channels = own_feats.shape[-1]
    context = own_feats.reshape(samples_dev, -1, channels)
    positions = context.shape[1]
    seg_len = depth_w.shape[1] // NSEG
    slot_total = block_cells.shape[-1]
    pos_groups = positions // BLK
    block_count = pos_groups * NSEG
    logits = jnp.dot(context.reshape(-1, channels), depth_w, preferred_element_type=jnp.float32)
    depth_prob = jax.nn.softmax(BOUND * jnp.tanh(logits / BOUND), axis=-1)
    depth_blocks = (
        depth_prob.reshape(samples_dev, pos_groups, BLK, NSEG, seg_len)
        .transpose(0, 1, 3, 2, 4)
        .reshape(samples_dev, block_count, BLK, seg_len)
    )
    slot_blocks = point_slot.reshape(samples_dev, block_count, BLK, seg_len)
    splat_w = jnp.stack(
        [
            jnp.sum(
                jnp.where(slot_blocks == target, depth_blocks, jnp.zeros_like(depth_blocks)),
                axis=-1,
            )
            for target in range(slot_total)
        ],
        axis=2,
    ).astype(jnp.bfloat16)
    block_ctx = jnp.repeat(context.reshape(samples_dev, pos_groups, BLK, channels), NSEG, axis=1)
    row_count = cotangent.shape[2]
    col_count = cotangent.shape[3]
    cells_tile = row_count * col_count
    capacity = max(2, 4 * block_count // tile_count)
    targets = block_tile.reshape(samples_dev, block_count)
    member = (targets[..., None] == jnp.arange(tile_count, dtype=jnp.int32)).astype(jnp.int32)
    slot_rank = jnp.sum((jnp.cumsum(member, axis=1) - 1) * member, axis=-1)
    slot_flat = targets * capacity + slot_rank
    sample_rows = jnp.broadcast_to(
        jnp.arange(samples_dev, dtype=jnp.int32)[:, None], slot_flat.shape
    )
    send_ctx = (
        jnp.zeros((samples_dev, tile_count * capacity, BLK, channels), jnp.bfloat16)
        .at[sample_rows, slot_flat]
        .set(block_ctx)
    )
    send_weights = (
        jnp.zeros((samples_dev, tile_count * capacity, slot_total, BLK), jnp.bfloat16)
        .at[sample_rows, slot_flat]
        .set(splat_w)
    )
    send_cells = (
        jnp.full((samples_dev, tile_count * capacity, slot_total), cells_tile, jnp.int32)
        .at[sample_rows, slot_flat]
        .set(block_cells.reshape(samples_dev, block_count, slot_total))
    )
    send_ctx = send_ctx.reshape(samples_dev, tile_count, capacity, BLK, channels)
    send_weights = send_weights.reshape(samples_dev, tile_count, capacity, slot_total, BLK)
    send_cells = send_cells.reshape(samples_dev, tile_count, capacity, slot_total)
    got_ctx, got_weights, got_cells = (
        lax.all_to_all(send_ctx, "tile", split_axis=1, concat_axis=1, tiled=True),
        lax.all_to_all(send_weights, "tile", split_axis=1, concat_axis=1, tiled=True),
        lax.all_to_all(send_cells, "tile", split_axis=1, concat_axis=1, tiled=True),
    )
    pooled = jnp.einsum(
        "ankti,ankic->anktc", got_weights, got_ctx, preferred_element_type=jnp.float32
    ).astype(jnp.bfloat16)
    group_size = min(8, tile_count)
    group_count = tile_count // group_size
    group_rows = group_size * capacity * slot_total
    pooled_groups = jnp.moveaxis(
        pooled.reshape(samples_dev, group_count, group_rows, channels), 1, 0
    )
    cell_groups = jnp.moveaxis(got_cells.reshape(samples_dev, group_count, group_rows), 1, 0)
    cell_range = jnp.arange(cells_tile, dtype=jnp.int32).reshape(1, cells_tile, 1)

    def splat_group(grid_sum, pieces):
        part_pooled, part_cells = pieces
        one_hot = (part_cells[:, None, :] == cell_range).astype(jnp.bfloat16)
        grid_sum = grid_sum + jnp.einsum(
            "sxr,src->sxc", one_hot, part_pooled, preferred_element_type=jnp.float32
        )
        return (grid_sum, None)

    totals, _ = lax.scan(
        splat_group,
        jnp.zeros((samples_dev, cells_tile, channels), jnp.float32),
        (pooled_groups, cell_groups),
    )
    bev_grid = totals.astype(jnp.bfloat16).reshape(samples_dev, row_count, col_count, channels)
    padded_grid = extended(bev_grid, (("tile", 1),), 1)
    bev_patches = patches_from(padded_grid, row_count, col_count)
    mixed = jnp.dot(bev_patches, bev_w, preferred_element_type=jnp.float32)
    encoded = (
        (bev_grid.astype(jnp.float32).reshape(-1, channels) + mixed)
        .astype(jnp.bfloat16)
        .reshape(cotangent.shape)
    )
    upstream = cotangent.reshape(-1, channels)
    total_cells = (
        micro_all * cotangent.shape[1] * lax.axis_size("dp") * row_count * tile_count * col_count
    )
    grad_scale = float(total_cells) ** (-0.5)
    grad_share = lax.psum_scatter(
        grad_scale
        * lax.dot_general(
            upstream, bev_patches, (((0,), (0,)), ((), ())), preferred_element_type=jnp.float32
        ),
        "tile",
        scatter_dimension=0,
        tiled=True,
    )
    conv_grad = lax.psum(grad_share, ("phase", "dp"))
    return (encoded, conv_grad)


MESH = pl.DeviceIdType.MESH
NT = (((1,), (1,)), ((), ()))
TN = (((0,), (0,)), ((), ()))
F32 = jnp.float32
BF16 = jnp.bfloat16


def with_side_columns(block, width):
    rows = block.shape[0]
    wide = block.astype(F32)
    col = lax.broadcasted_iota(jnp.int32, block.shape, 0) % width
    before = jnp.where(col == 0, 0.0, pltpu.roll(wide, 1, 0))
    after = jnp.where(col == width - 1, 0.0, pltpu.roll(wide, rows - 1, 0))
    return before.astype(BF16), block, after.astype(BF16)


def fused_kernel(
    dims,
    cam_ref, w_ref, dw_ref, slots_ref, code_ref, bw_ref, cot_ref,
    enc_ref, grad_ref,
    x_ref, z_ref, wall_ref, codes_ref, acc_w, wt_ref, back_ref, same_ref, up_ref, acc_ref, zb_ref,
    gpart, gsend, grecv_a, gsum, gsend_b, grecv_b, grecv_c, gfin, gfin_other,
    local_sem, row_send, row_recv, code_send, code_recv, w_send, w_recv, f_send, f_recv,
    wt_send, wt_recv, a_send, a_recv, b_send, b_recv, c_send, c_recv, d_send, d_recv,
):
    phases, tiles, width, slots, bins, seg, grid_rows, grid_cols, scale = dims
    ph, ti, dp = lax.axis_index("phase"), lax.axis_index("tile"), lax.axis_index("dp")
    other = 1 - dp
    pos = cam_ref.shape[1]
    channels = cam_ref.shape[2]
    lanes = code_ref.shape[1]
    half = w_ref.shape[0] // 2
    cols3 = 3 * channels

    def tile_peer(k):
        return (ph, lax.rem(ti + k, tiles), dp)

    def phase_peer(k):
        return (lax.rem(ph + k, phases), ti, dp)

    partner = (ph, ti, other)

    barrier = pltpu.get_barrier_semaphore()
    for k in range(1, tiles):
        pl.semaphore_signal(barrier, inc=1, device_id=tile_peer(k), device_id_type=MESH)
    for k in range(1, phases):
        pl.semaphore_signal(barrier, inc=1, device_id=phase_peer(k), device_id_type=MESH)
    pl.semaphore_signal(barrier, inc=1, device_id=partner, device_id_type=MESH)
    pl.semaphore_wait(barrier, tiles - 1 + phases - 1 + 1)

    def remote(src, dst, send, recv, device):
        copy = pltpu.make_async_remote_copy(
            src_ref=src, dst_ref=dst, send_sem=send, recv_sem=recv,
            device_id=device, device_id_type=MESH,
        )
        copy.start()
        return copy

    own_rows = pl.ds(pl.multiple_of(ti * pos, 16), pos)
    own_lanes = pl.ds(pl.multiple_of(ti * lanes, 128), lanes)
    own_half = pl.ds(pl.multiple_of(dp * half, 16), half)
    w_copies = [
        remote(w_ref.at[own_half], wall_ref.at[ph, own_half], w_send.at[k], w_recv.at[k], phase_peer(k))
        for k in range(1, phases)
    ]
    row_copies = [
        remote(cam_ref.at[ph], x_ref.at[own_rows], row_send.at[k], row_recv.at[k], tile_peer(k))
        for k in range(1, tiles)
    ]
    code_copies = [
        remote(code_ref, codes_ref.at[:, own_lanes], code_send.at[k], code_recv.at[k], tile_peer(k))
        for k in range(1, tiles)
    ]
    own = [
        pltpu.make_async_copy(cam_ref.at[ph], x_ref.at[own_rows], local_sem.at[0]),
        pltpu.make_async_copy(code_ref, codes_ref.at[:, own_lanes], local_sem.at[1]),
        pltpu.make_async_copy(w_ref, wall_ref.at[ph], local_sem.at[2]),
    ]
    for copy in own:
        copy.start()

    edge = jnp.zeros((pos, cols3), BF16)
    z_ref[pl.ds(0, pos), :] = edge
    z_ref[pl.ds((tiles + 1) * pos, pos), :] = edge
    acc_ref[...] = jnp.zeros_like(acc_ref)
    acc_w[...] = jnp.zeros_like(acc_w)

    up_ref[...] = cot_ref[...].astype(F32).T.astype(BF16)
    forwards = []
    for k in range(1, phases):
        w_copies[k - 1].wait_recv()
        source = lax.rem(ph - k + phases, phases)
        forwards.append(
            remote(wall_ref.at[source, own_half], wall_ref.at[source, own_half],
                   f_send.at[k], f_recv.at[k], partner)
        )
    for copy in own + row_copies + code_copies + forwards:
        copy.wait()
    for copy in w_copies:
        copy.wait_send()

    @pl.loop(0, phases)
    def _(s):
        @pl.loop(0, tiles, unroll=2)
        def _(u):
            rows = x_ref[pl.ds(pl.multiple_of(u * pos, 16), pos), :]
            at = pl.ds(pl.multiple_of((u + 1) * pos, 16), pos)
            for e, part in enumerate(with_side_columns(rows, width)):
                z_ref[at, e * channels : (e + 1) * channels] = part

        @pl.loop(0, tiles, unroll=2)
        def _(u):
            at = pl.ds(pl.multiple_of(u * pos, 16), pos)
            patches = jnp.concatenate(
                [z_ref[pl.ds(pl.multiple_of((u + a) * pos, 16), pos), :] for a in range(3)], axis=1
            )
            hidden = jnp.dot(patches, wall_ref[s], preferred_element_type=F32)
            x_ref[at, :] = (x_ref[at, :].astype(F32) + hidden * jax.nn.sigmoid(hidden)).astype(BF16)

    logits = jnp.dot(x_ref[own_rows, :], dw_ref[...], preferred_element_type=F32)
    lane = lax.broadcasted_iota(jnp.int32, logits.shape, 1)
    inside = (lane % 128) < seg
    raised = jnp.where(inside, jnp.exp(BOUND * jnp.tanh(logits / BOUND)), 0.0)
    prob = raised / jnp.sum(raised, axis=1, keepdims=True)
    half_of = lax.broadcasted_iota(jnp.int32, (bins, 128), 0) // 128
    target_col = lax.broadcasted_iota(jnp.int32, (bins, 128), 1)
    summed = jnp.zeros((pos, 128), F32)
    for t in range(slots):
        chosen = jnp.where(slots_ref[...] == t, prob, 0.0).astype(BF16)
        into = jnp.where(target_col == half_of * slots + t, 1.0, 0.0).astype(BF16)
        summed += jnp.dot(chosen, into, preferred_element_type=F32)
    acc_w[pl.ds(0, pos), :] = summed.astype(BF16)
    names = NSEG * slots
    pick = jnp.where(
        lax.broadcasted_iota(jnp.int32, (names, 128), 0) == lax.broadcasted_iota(jnp.int32, (names, 128), 1),
        1.0, 0.0,
    ).astype(BF16)
    wt_ref[ti] = lax.dot_general(pick, acc_w[...], NT, preferred_element_type=F32).astype(BF16)
    for k in range(1, tiles):
        remote(wt_ref.at[ti], wt_ref.at[ti], wt_send.at[k], wt_recv.at[k], tile_peer(k))

    chunk_pos = width
    chunk_rows = chunk_pos // BLK * names
    spread = jnp.where(
        lax.broadcasted_iota(jnp.int32, (names, chunk_rows), 1) % names
        == lax.broadcasted_iota(jnp.int32, (names, chunk_rows), 0),
        1.0, 0.0,
    ).astype(BF16)
    shape = (chunk_pos, chunk_rows)
    same_ref[...] = jnp.where(
        lax.broadcasted_iota(jnp.int32, shape, 0) // BLK == lax.broadcasted_iota(jnp.int32, shape, 1) // names,
        1.0, 0.0,
    ).astype(BF16)
    window = grid_rows + 2

    def add_blocks(u):
        back_ref[...] = wt_ref[u].astype(F32).T.astype(BF16)

        @pl.loop(0, pos // chunk_pos)
        def _(c):
            here = pl.ds(pl.multiple_of(c * chunk_pos, 16), chunk_pos)
            at = pl.ds(pl.multiple_of(u * pos + c * chunk_pos, 16), chunk_pos)
            tiled = jnp.dot(back_ref[here, :], spread, preferred_element_type=F32)
            weights = tiled.astype(BF16) * same_ref[...]
            pooled = lax.dot_general(x_ref[at, :], weights, TN, preferred_element_type=F32).astype(BF16)
            cell = codes_ref[:, pl.ds(pl.multiple_of(u * lanes + c * chunk_rows, 128), chunk_rows)]
            cell = cell - (ti * grid_rows - 1) * grid_cols
            row = cell >> 8
            column = cell & (grid_cols - 1)
            marks = jnp.where(
                lax.broadcasted_iota(jnp.int32, (grid_cols, chunk_rows), 0) == column, 1.0, 0.0
            ).astype(BF16)
            parts = [pooled * jnp.where(row == y, 1.0, 0.0).astype(BF16) for y in range(window)]
            acc_ref[...] += lax.dot_general(
                jnp.concatenate(parts, axis=0), marks, NT, preferred_element_type=F32
            )

    @pl.loop(0, tiles)
    def _(d):
        @pl.when(d > 0)
        def _():
            pltpu.make_async_remote_copy(
                src_ref=wt_ref.at[ti], dst_ref=wt_ref.at[ti],
                send_sem=wt_send.at[d], recv_sem=wt_recv.at[d],
                device_id=tile_peer(d), device_id_type=MESH,
            ).wait()

        add_blocks(lax.rem(ti + tiles - d, tiles))

    for y in range(window):
        line = acc_ref[y * channels : (y + 1) * channels, :].T.astype(BF16)
        for e, part in enumerate(with_side_columns(line, grid_cols)):
            zb_ref[y * grid_cols : (y + 1) * grid_cols, e * channels : (e + 1) * channels] = part

    cells = grid_rows * grid_cols
    for a in range(3):
        term = scale * jnp.dot(
            up_ref[...], zb_ref[a * grid_cols : a * grid_cols + cells, :], preferred_element_type=F32
        )
        for t in range(tiles):
            for d in range(2):
                piece = term[(2 * t + d) * 16 : (2 * t + d + 1) * 16]
                gpart[d, t, :, a * cols3 : (a + 1) * cols3] = piece
                gsend[d, t, :, a * cols3 : (a + 1) * cols3] = piece.astype(BF16)
    to_partner = remote(gsend.at[other], grecv_a, a_send, a_recv, partner)

    def encode(y):
        patches = jnp.concatenate(
            [zb_ref[(y + a) * grid_cols : (y + a + 1) * grid_cols, :] for a in range(3)], axis=1
        )
        own_row = zb_ref[(y + 1) * grid_cols : (y + 2) * grid_cols, channels : 2 * channels]
        mixed = own_row.astype(F32) + jnp.dot(patches, bw_ref[...], preferred_element_type=F32)
        enc_ref[y * grid_cols : (y + 1) * grid_cols, :] = mixed.astype(BF16)

    quarter = grid_rows // 4
    for y in range(quarter):
        encode(y)
    to_partner.wait()
    for t in range(tiles):
        total = gpart[dp, t] + grecv_a[t].astype(F32)
        gsum[t] = total
        gsend_b[t] = total.astype(BF16)
    b_copies = [
        remote(gsend_b.at[lax.rem(ti + k, tiles)], grecv_b.at[ti], b_send.at[k], b_recv.at[k], tile_peer(k))
        for k in range(1, tiles)
    ]
    for y in range(quarter, 3 * quarter):
        encode(y)
    for copy in b_copies:
        copy.wait()
    total = gsum[ti]
    for k in range(1, tiles):
        total += grecv_b[lax.rem(ti + k, tiles)].astype(F32)
    grecv_c[ph] = total.astype(BF16)
    c_copies = [
        remote(grecv_c.at[ph], grecv_c.at[ph], c_send.at[k], c_recv.at[k], phase_peer(k))
        for k in range(1, phases)
    ]
    for y in range(3 * quarter, grid_rows):
        encode(y)
    for copy in c_copies:
        copy.wait()
    total = grecv_c[0].astype(F32)
    for p in range(1, phases):
        total += grecv_c[p].astype(F32)
    gfin[...] = total
    last = remote(gfin, gfin_other, d_send, d_recv, partner)
    grad_ref[dp] = total
    last.wait()
    grad_ref[other] = gfin_other[...]


def fused_body(camera_feats, backbone_w, depth_w, block_tile, point_slot, block_cells, bev_w, cotangent):
    phases, tiles = lax.axis_size("phase"), lax.axis_size("tile")
    micro, _, cams, _, width, channels = camera_feats.shape
    pos = cams * width
    groups = pos // BLK
    seg = depth_w.shape[1] // NSEG
    slots = block_cells.shape[-1]
    grid_rows, grid_cols = cotangent.shape[2:4]
    cells = grid_rows * grid_cols
    side = [(0, 0), (0, 0), (0, 128 - seg)]
    bins = NSEG * 128
    heads = jnp.pad(depth_w.reshape(channels, NSEG, seg), side).reshape(channels, bins)
    point = point_slot.reshape(groups, NSEG, BLK, seg).transpose(0, 2, 1, 3).reshape(pos, NSEG, seg)
    point = jnp.pad(point, side).reshape(pos, bins)
    local = block_cells.reshape(groups * NSEG, slots)
    code = block_tile.reshape(groups * NSEG, 1) * cells + local
    code = jnp.where(local < cells, code, 1 << 24).reshape(1, groups * NSEG * slots)
    total = micro * cotangent.shape[1] * lax.axis_size("dp") * cells * tiles
    dims = (phases, tiles, width, slots, bins, seg, grid_rows, grid_cols, float(total) ** (-0.5))
    rows = code.shape[1]
    cols = 9 * channels
    pad_pos = -(-pos // 128) * 128
    dma = pltpu.SemaphoreType.DMA
    vmem = pl.BlockSpec(memory_space=pltpu.VMEM)
    scratch = [
        pltpu.VMEM((tiles * pos, channels), BF16),
        pltpu.VMEM(((tiles + 2) * pos, 3 * channels), BF16),
        pltpu.VMEM((phases, cols, channels), BF16),
        pltpu.VMEM((1, tiles * rows), jnp.int32),
        pltpu.VMEM((pad_pos, 128), BF16),
        pltpu.VMEM((tiles, NSEG * slots, pad_pos), BF16),
        pltpu.VMEM((pad_pos, NSEG * slots), BF16),
        pltpu.VMEM((width, width // BLK * NSEG * slots), BF16),
        pltpu.VMEM((channels, cells), BF16),
        pltpu.VMEM(((grid_rows + 2) * channels, grid_cols), F32),
        pltpu.VMEM(((grid_rows + 2) * grid_cols, 3 * channels), BF16),
        pltpu.VMEM((2, tiles, 16, cols), F32),
        pltpu.VMEM((2, tiles, 16, cols), BF16),
        pltpu.VMEM((tiles, 16, cols), BF16),
        pltpu.VMEM((tiles, 16, cols), F32),
        pltpu.VMEM((tiles, 16, cols), BF16),
        pltpu.VMEM((tiles, 16, cols), BF16),
        pltpu.VMEM((phases, 16, cols), BF16),
        pltpu.VMEM((16, cols), F32),
        pltpu.VMEM((16, cols), F32),
        dma((3,)),
        dma((tiles,)), dma((tiles,)), dma((tiles,)), dma((tiles,)),
        dma((phases,)), dma((phases,)), dma((phases,)), dma((phases,)),
        dma((tiles,)), dma((tiles,)),
        dma(()), dma(()),
        dma((tiles,)), dma((tiles,)),
        dma((phases,)), dma((phases,)),
        dma(()), dma(()),
    ]
    encoded, grad = pl.pallas_call(
        functools.partial(fused_kernel, dims),
        out_shape=(
            jax.ShapeDtypeStruct((cells, channels), BF16),
            jax.ShapeDtypeStruct((2, 16, cols), F32),
        ),
        in_specs=[vmem] * 7,
        out_specs=(vmem, vmem),
        scratch_shapes=scratch,
        compiler_params=pltpu.CompilerParams(
            collective_id=0, has_side_effects=True, vmem_limit_bytes=48 * 1024 * 1024
        ),
        name="lift_splat",
    )(
        camera_feats.reshape(micro, pos, channels),
        backbone_w[0],
        heads,
        point,
        code,
        bev_w,
        cotangent.reshape(cells, channels),
    )
    return encoded.reshape(cotangent.shape), grad.reshape(32, cols)


def solution(mesh):
    return jax.shard_map(
        fused_body if mesh.shape["tile"] == 4 else body,
        mesh=mesh,
        in_specs=(
            P(None, "dp", None, "tile", None, None),
            P("phase", None, None),
            P(),
            P("phase", "dp", "tile", None),
            P("phase", "dp", "tile", None),
            P("phase", "dp", "tile", None),
            P(),
            P("phase", "dp", "tile", None, None),
        ),
        out_specs=(P("phase", "dp", "tile", None, None), P("tile", None)),
        check_vma=False,
    )
```

```python
import functools

import jax
import jax.numpy as jnp
from jax import lax
from jax.experimental import pallas as pl
from jax.experimental.pallas import tpu as pltpu
from jax.sharding import PartitionSpec as P

NSEG = 2
BLK = 4


BOUND = 8.0


def extended(cells, sides, width):
    for axis, dim in sides:
        count = lax.axis_size(axis)
        ends = count - 1
        head = lax.slice_in_dim(cells, 0, width, axis=dim)
        tail = lax.slice_in_dim(cells, cells.shape[dim] - width, cells.shape[dim], axis=dim)
        cells = jnp.concatenate(
            [
                lax.ppermute(tail, axis, [(i, (i + 1) % count) for i in range(ends)]),
                cells,
                lax.ppermute(head, axis, [((i + 1) % count, i) for i in range(ends)]),
            ],
            axis=dim,
        )
    return cells


def passed_along(block, axis, distance):
    devices = range(lax.axis_size(axis))
    route = [(i - distance, i) for i in devices if i - distance in devices]
    return lax.ppermute(block, axis, route)


def from_root(block, axis, source):
    block = jnp.where(lax.axis_index(axis) == source, block, jnp.zeros_like(block))
    return lax.psum(block, axis)


def patches_from(padded, row_count, col_count):
    widened = jnp.pad(padded, [(0, 0)] * (padded.ndim - 2) + [(1, 1), (0, 0)])
    shifted = [
        widened[..., row_off : row_off + row_count, col_off : col_off + col_count, :]
        for row_off in range(3)
        for col_off in range(3)
    ]
    stacked = jnp.concatenate(shifted, axis=-1)
    return stacked.reshape(-1, stacked.shape[-1])


def section(images, weight):
    padded = extended(images, (("tile", 2),), 1)
    hidden = jnp.dot(
        patches_from(padded, images.shape[2], images.shape[3]),
        weight,
        preferred_element_type=jnp.float32,
    ).reshape(images.shape)
    return (images.astype(jnp.float32) + jax.nn.silu(hidden)).astype(jnp.bfloat16)


def body(camera_feats, backbone_w, depth_w, block_tile, point_slot, block_cells, bev_w, cotangent):
    phases = lax.axis_size("phase")
    phase_idx = lax.axis_index("phase")
    tile_count = lax.axis_size("tile")
    micro_all = camera_feats.shape[0]
    per_phase = micro_all // phases
    own_weight = backbone_w[0]
    carried = jnp.zeros_like(camera_feats[0])
    collected = jnp.zeros_like(camera_feats)
    steps_total = micro_all + phases - 1
    for step_idx in range(steps_total):
        if step_idx < micro_all:
            entering = jnp.where(phase_idx == 0, camera_feats[step_idx], carried)
        else:
            entering = carried
        leaving = section(entering, own_weight)
        finished = step_idx - (phases - 1)
        if finished >= 0:
            collected = collected.at[finished].set(
                jnp.where(phase_idx == phases - 1, leaving, collected[finished])
            )
        if step_idx + 1 < steps_total:
            carried = passed_along(leaving, "phase", 1)
    everything = from_root(collected, "phase", phases - 1)
    own_feats = lax.dynamic_slice_in_dim(everything, phase_idx * per_phase, per_phase, 0)
    samples_dev = own_feats.shape[0] * own_feats.shape[1]
    channels = own_feats.shape[-1]
    context = own_feats.reshape(samples_dev, -1, channels)
    positions = context.shape[1]
    seg_len = depth_w.shape[1] // NSEG
    slot_total = block_cells.shape[-1]
    pos_groups = positions // BLK
    block_count = pos_groups * NSEG
    logits = jnp.dot(context.reshape(-1, channels), depth_w, preferred_element_type=jnp.float32)
    depth_prob = jax.nn.softmax(BOUND * jnp.tanh(logits / BOUND), axis=-1)
    depth_blocks = (
        depth_prob.reshape(samples_dev, pos_groups, BLK, NSEG, seg_len)
        .transpose(0, 1, 3, 2, 4)
        .reshape(samples_dev, block_count, BLK, seg_len)
    )
    slot_blocks = point_slot.reshape(samples_dev, block_count, BLK, seg_len)
    splat_w = jnp.stack(
        [
            jnp.sum(
                jnp.where(slot_blocks == target, depth_blocks, jnp.zeros_like(depth_blocks)),
                axis=-1,
            )
            for target in range(slot_total)
        ],
        axis=2,
    ).astype(jnp.bfloat16)
    block_ctx = jnp.repeat(context.reshape(samples_dev, pos_groups, BLK, channels), NSEG, axis=1)
    row_count = cotangent.shape[2]
    col_count = cotangent.shape[3]
    cells_tile = row_count * col_count
    capacity = max(2, 4 * block_count // tile_count)
    targets = block_tile.reshape(samples_dev, block_count)
    member = (targets[..., None] == jnp.arange(tile_count, dtype=jnp.int32)).astype(jnp.int32)
    slot_rank = jnp.sum((jnp.cumsum(member, axis=1) - 1) * member, axis=-1)
    slot_flat = targets * capacity + slot_rank
    sample_rows = jnp.broadcast_to(
        jnp.arange(samples_dev, dtype=jnp.int32)[:, None], slot_flat.shape
    )
    send_ctx = (
        jnp.zeros((samples_dev, tile_count * capacity, BLK, channels), jnp.bfloat16)
        .at[sample_rows, slot_flat]
        .set(block_ctx)
    )
    send_weights = (
        jnp.zeros((samples_dev, tile_count * capacity, slot_total, BLK), jnp.bfloat16)
        .at[sample_rows, slot_flat]
        .set(splat_w)
    )
    send_cells = (
        jnp.full((samples_dev, tile_count * capacity, slot_total), cells_tile, jnp.int32)
        .at[sample_rows, slot_flat]
        .set(block_cells.reshape(samples_dev, block_count, slot_total))
    )
    send_ctx = send_ctx.reshape(samples_dev, tile_count, capacity, BLK, channels)
    send_weights = send_weights.reshape(samples_dev, tile_count, capacity, slot_total, BLK)
    send_cells = send_cells.reshape(samples_dev, tile_count, capacity, slot_total)
    got_ctx, got_weights, got_cells = (
        lax.all_to_all(send_ctx, "tile", split_axis=1, concat_axis=1, tiled=True),
        lax.all_to_all(send_weights, "tile", split_axis=1, concat_axis=1, tiled=True),
        lax.all_to_all(send_cells, "tile", split_axis=1, concat_axis=1, tiled=True),
    )
    pooled = jnp.einsum(
        "ankti,ankic->anktc", got_weights, got_ctx, preferred_element_type=jnp.float32
    ).astype(jnp.bfloat16)
    group_size = min(8, tile_count)
    group_count = tile_count // group_size
    group_rows = group_size * capacity * slot_total
    pooled_groups = jnp.moveaxis(
        pooled.reshape(samples_dev, group_count, group_rows, channels), 1, 0
    )
    cell_groups = jnp.moveaxis(got_cells.reshape(samples_dev, group_count, group_rows), 1, 0)
    cell_range = jnp.arange(cells_tile, dtype=jnp.int32).reshape(1, cells_tile, 1)

    def splat_group(grid_sum, pieces):
        part_pooled, part_cells = pieces
        one_hot = (part_cells[:, None, :] == cell_range).astype(jnp.bfloat16)
        grid_sum = grid_sum + jnp.einsum(
            "sxr,src->sxc", one_hot, part_pooled, preferred_element_type=jnp.float32
        )
        return (grid_sum, None)

    totals, _ = lax.scan(
        splat_group,
        jnp.zeros((samples_dev, cells_tile, channels), jnp.float32),
        (pooled_groups, cell_groups),
    )
    bev_grid = totals.astype(jnp.bfloat16).reshape(samples_dev, row_count, col_count, channels)
    padded_grid = extended(bev_grid, (("tile", 1),), 1)
    bev_patches = patches_from(padded_grid, row_count, col_count)
    mixed = jnp.dot(bev_patches, bev_w, preferred_element_type=jnp.float32)
    encoded = (
        (bev_grid.astype(jnp.float32).reshape(-1, channels) + mixed)
        .astype(jnp.bfloat16)
        .reshape(cotangent.shape)
    )
    upstream = cotangent.reshape(-1, channels)
    total_cells = (
        micro_all * cotangent.shape[1] * lax.axis_size("dp") * row_count * tile_count * col_count
    )
    grad_scale = float(total_cells) ** (-0.5)
    grad_share = lax.psum_scatter(
        grad_scale
        * lax.dot_general(
            upstream, bev_patches, (((0,), (0,)), ((), ())), preferred_element_type=jnp.float32
        ),
        "tile",
        scatter_dimension=0,
        tiled=True,
    )
    conv_grad = lax.psum(grad_share, ("phase", "dp"))
    return (encoded, conv_grad)


MESH = pl.DeviceIdType.MESH
NT = (((1,), (1,)), ((), ()))
TN = (((0,), (0,)), ((), ()))
F32 = jnp.float32
BF16 = jnp.bfloat16


def with_side_columns(block, width):
    rows = block.shape[0]
    wide = block.astype(F32)
    col = lax.broadcasted_iota(jnp.int32, block.shape, 0) % width
    before = jnp.where(col == 0, 0.0, pltpu.roll(wide, 1, 0))
    after = jnp.where(col == width - 1, 0.0, pltpu.roll(wide, rows - 1, 0))
    return before.astype(BF16), block, after.astype(BF16)


def fused_kernel(
    dims,
    cam_ref, w_ref, dw_ref, slots_ref, code_ref, bw_ref, cot_ref,
    enc_ref, grad_ref,
    x_ref, z_ref, wall_ref, codes_ref, acc_w, wt_ref, back_ref, same_ref, up_ref, acc_ref, zb_ref,
    gpart, gsend, grecv_a, gsum, gsend_b, grecv_b, grecv_c, gfin, gfin_other,
    local_sem, row_send, row_recv, code_send, code_recv, w_send, w_recv, f_send, f_recv,
    wt_send, wt_recv, a_send, a_recv, b_send, b_recv, c_send, c_recv, d_send, d_recv,
):
    phases, tiles, width, slots, bins, seg, grid_rows, grid_cols, scale = dims
    ph, ti, dp = lax.axis_index("phase"), lax.axis_index("tile"), lax.axis_index("dp")
    other = 1 - dp
    pos = cam_ref.shape[1]
    channels = cam_ref.shape[2]
    lanes = code_ref.shape[1]
    half = w_ref.shape[0] // 2
    cols3 = 3 * channels

    def tile_peer(k):
        return (ph, lax.rem(ti + k, tiles), dp)

    def phase_peer(k):
        return (lax.rem(ph + k, phases), ti, dp)

    partner = (ph, ti, other)

    barrier = pltpu.get_barrier_semaphore()
    for k in range(1, tiles):
        pl.semaphore_signal(barrier, inc=1, device_id=tile_peer(k), device_id_type=MESH)
    for k in range(1, phases):
        pl.semaphore_signal(barrier, inc=1, device_id=phase_peer(k), device_id_type=MESH)
    pl.semaphore_signal(barrier, inc=1, device_id=partner, device_id_type=MESH)
    pl.semaphore_wait(barrier, tiles - 1 + phases - 1 + 1)

    def remote(src, dst, send, recv, device):
        copy = pltpu.make_async_remote_copy(
            src_ref=src, dst_ref=dst, send_sem=send, recv_sem=recv,
            device_id=device, device_id_type=MESH,
        )
        copy.start()
        return copy

    own_rows = pl.ds(pl.multiple_of(ti * pos, 16), pos)
    own_lanes = pl.ds(pl.multiple_of(ti * lanes, 128), lanes)
    own_half = pl.ds(pl.multiple_of(dp * half, 16), half)
    w_copies = [
        remote(w_ref.at[own_half], wall_ref.at[ph, own_half], w_send.at[k], w_recv.at[k], phase_peer(k))
        for k in range(1, phases)
    ]
    cams = pos // width

    def piece(row, c):
        return pl.ds(pl.multiple_of(row * pos + c * width, 16), width)

    def hop(row, c, step):
        return pltpu.make_async_remote_copy(
            src_ref=x_ref.at[piece(row, c)], dst_ref=x_ref.at[piece(row, c)],
            send_sem=row_send.at[(step + 1) // 2, row, c], recv_sem=row_recv.at[row, c],
            device_id=(ph, ti + step, dp), device_id_type=MESH,
        )

    def own_hop(c, step):
        return pltpu.make_async_remote_copy(
            src_ref=cam_ref.at[ph, c * width : (c + 1) * width], dst_ref=x_ref.at[piece(ti, c)],
            send_sem=row_send.at[(step + 1) // 2, ti, c], recv_sem=row_recv.at[ti, c],
            device_id=(ph, ti + step, dp), device_id_type=MESH,
        )

    def relay(act_own, act):
        for c in range(cams):
            for step in (1, -1):
                if act_own is not None:
                    @pl.when((ti + step >= 0) & (ti + step < tiles))
                    def _():
                        act_own(own_hop(c, step))
        for d in act:
            for c in range(cams):
                for step in (1, -1):
                    source = ti - step * d
                    @pl.when((source >= 0) & (source < tiles))
                    def _():
                        if act_own is None:
                            hop(source, c, -step).wait_recv()

                        @pl.when((ti + step >= 0) & (ti + step < tiles))
                        def _():
                            if act_own is None:
                                hop(source, c, step).start()
                            else:
                                hop(source, c, step).wait_send()

    relay(lambda copy: copy.start(), ())
    own = [
        pltpu.make_async_copy(cam_ref.at[ph], x_ref.at[own_rows], local_sem.at[0]),
        pltpu.make_async_copy(code_ref, codes_ref.at[:, own_lanes], local_sem.at[1]),
        pltpu.make_async_copy(w_ref, wall_ref.at[ph], local_sem.at[2]),
    ]
    for copy in own:
        copy.start()
    relay(None, (1,))

    edge = jnp.zeros((pos, cols3), BF16)
    z_ref[pl.ds(0, pos), :] = edge
    z_ref[pl.ds((tiles + 1) * pos, pos), :] = edge
    acc_ref[...] = jnp.zeros_like(acc_ref)
    acc_w[...] = jnp.zeros_like(acc_w)

    up_ref[...] = cot_ref[...].astype(F32).T.astype(BF16)
    relay(None, range(2, tiles - 1))
    forwards = []
    for k in range(1, phases):
        w_copies[k - 1].wait_recv()
        source = lax.rem(ph - k + phases, phases)
        forwards.append(
            remote(wall_ref.at[source, own_half], wall_ref.at[source, own_half],
                   f_send.at[k], f_recv.at[k], partner)
        )
    relay(None, (tiles - 1,))
    for copy in own + forwards:
        copy.wait()
    relay(lambda copy: copy.wait_send(), range(1, tiles))
    code_copies = [
        remote(code_ref, codes_ref.at[:, own_lanes], code_send.at[k], code_recv.at[k], tile_peer(k))
        for k in range(1, tiles)
    ]
    for copy in w_copies:
        copy.wait_send()

    @pl.loop(0, phases)
    def _(s):
        @pl.loop(0, tiles, unroll=4)
        def _(u):
            rows = x_ref[pl.ds(pl.multiple_of(u * pos, 16), pos), :]
            at = pl.ds(pl.multiple_of((u + 1) * pos, 16), pos)
            for e, part in enumerate(with_side_columns(rows, width)):
                z_ref[at, e * channels : (e + 1) * channels] = part

        @pl.loop(0, tiles, unroll=4)
        def _(u):
            at = pl.ds(pl.multiple_of(u * pos, 16), pos)
            patches = jnp.concatenate(
                [z_ref[pl.ds(pl.multiple_of((u + a) * pos, 16), pos), :] for a in range(3)], axis=1
            )
            hidden = jnp.dot(patches, wall_ref[s], preferred_element_type=F32)
            x_ref[at, :] = (x_ref[at, :].astype(F32) + hidden * jax.nn.sigmoid(hidden)).astype(BF16)

    logits = jnp.dot(x_ref[own_rows, :], dw_ref[...], preferred_element_type=F32)
    lane = lax.broadcasted_iota(jnp.int32, logits.shape, 1)
    inside = (lane % 128) < seg
    raised = jnp.where(inside, jnp.exp(BOUND * jnp.tanh(logits / BOUND)), 0.0)
    prob = raised / jnp.sum(raised, axis=1, keepdims=True)
    half_of = lax.broadcasted_iota(jnp.int32, (bins, 128), 0) // 128
    target_col = lax.broadcasted_iota(jnp.int32, (bins, 128), 1)
    summed = jnp.zeros((pos, 128), F32)
    for t in range(slots):
        chosen = jnp.where(slots_ref[...] == t, prob, 0.0).astype(BF16)
        into = jnp.where(target_col == half_of * slots + t, 1.0, 0.0).astype(BF16)
        summed += jnp.dot(chosen, into, preferred_element_type=F32)
    acc_w[pl.ds(0, pos), :] = summed.astype(BF16)
    names = NSEG * slots
    pick = jnp.where(
        lax.broadcasted_iota(jnp.int32, (names, 128), 0) == lax.broadcasted_iota(jnp.int32, (names, 128), 1),
        1.0, 0.0,
    ).astype(BF16)
    wt_ref[ti] = lax.dot_general(pick, acc_w[...], NT, preferred_element_type=F32).astype(BF16)
    for k in range(1, tiles):
        remote(wt_ref.at[ti], wt_ref.at[ti], wt_send.at[k], wt_recv.at[k], tile_peer(k))

    chunk_pos = width
    chunk_rows = chunk_pos // BLK * names
    spread = jnp.where(
        lax.broadcasted_iota(jnp.int32, (names, chunk_rows), 1) % names
        == lax.broadcasted_iota(jnp.int32, (names, chunk_rows), 0),
        1.0, 0.0,
    ).astype(BF16)
    shape = (chunk_pos, chunk_rows)
    same_ref[...] = jnp.where(
        lax.broadcasted_iota(jnp.int32, shape, 0) // BLK == lax.broadcasted_iota(jnp.int32, shape, 1) // names,
        1.0, 0.0,
    ).astype(BF16)
    window = grid_rows + 2

    for copy in code_copies:
        copy.wait()

    def add_blocks(u):
        back_ref[...] = wt_ref[u].astype(F32).T.astype(BF16)

        @pl.loop(0, pos // chunk_pos)
        def _(c):
            here = pl.ds(pl.multiple_of(c * chunk_pos, 16), chunk_pos)
            at = pl.ds(pl.multiple_of(u * pos + c * chunk_pos, 16), chunk_pos)
            tiled = jnp.dot(back_ref[here, :], spread, preferred_element_type=F32)
            weights = tiled.astype(BF16) * same_ref[...]
            pooled = lax.dot_general(x_ref[at, :], weights, TN, preferred_element_type=F32).astype(BF16)
            cell = codes_ref[:, pl.ds(pl.multiple_of(u * lanes + c * chunk_rows, 128), chunk_rows)]
            cell = cell - (ti * grid_rows - 1) * grid_cols
            row = cell >> 8
            column = cell & (grid_cols - 1)
            marks = jnp.where(
                lax.broadcasted_iota(jnp.int32, (grid_cols, chunk_rows), 0) == column, 1.0, 0.0
            ).astype(BF16)
            parts = [pooled * jnp.where(row == y, 1.0, 0.0).astype(BF16) for y in range(window)]
            acc_ref[...] += lax.dot_general(
                jnp.concatenate(parts, axis=0), marks, NT, preferred_element_type=F32
            )

    @pl.loop(0, tiles)
    def _(d):
        @pl.when(d > 0)
        def _():
            pltpu.make_async_remote_copy(
                src_ref=wt_ref.at[ti], dst_ref=wt_ref.at[ti],
                send_sem=wt_send.at[d], recv_sem=wt_recv.at[d],
                device_id=tile_peer(d), device_id_type=MESH,
            ).wait()

        add_blocks(lax.rem(ti + tiles - d, tiles))

    for y in range(window):
        line = acc_ref[y * channels : (y + 1) * channels, :].T.astype(BF16)
        for e, part in enumerate(with_side_columns(line, grid_cols)):
            zb_ref[y * grid_cols : (y + 1) * grid_cols, e * channels : (e + 1) * channels] = part

    cells = grid_rows * grid_cols
    for a in range(3):
        term = scale * jnp.dot(
            up_ref[...], zb_ref[a * grid_cols : a * grid_cols + cells, :], preferred_element_type=F32
        )
        for t in range(tiles):
            for d in range(2):
                piece = term[(2 * t + d) * 16 : (2 * t + d + 1) * 16]
                gpart[d, t, :, a * cols3 : (a + 1) * cols3] = piece
                gsend[d, t, :, a * cols3 : (a + 1) * cols3] = piece.astype(BF16)
    to_partner = remote(gsend.at[other], grecv_a, a_send, a_recv, partner)

    def encode(y):
        patches = jnp.concatenate(
            [zb_ref[(y + a) * grid_cols : (y + a + 1) * grid_cols, :] for a in range(3)], axis=1
        )
        own_row = zb_ref[(y + 1) * grid_cols : (y + 2) * grid_cols, channels : 2 * channels]
        mixed = own_row.astype(F32) + jnp.dot(patches, bw_ref[...], preferred_element_type=F32)
        enc_ref[y * grid_cols : (y + 1) * grid_cols, :] = mixed.astype(BF16)

    quarter = grid_rows // 4
    for y in range(quarter):
        encode(y)
    to_partner.wait()
    for t in range(tiles):
        total = gpart[dp, t] + grecv_a[t].astype(F32)
        gsum[t] = total
        gsend_b[t] = total.astype(BF16)
    b_copies = [
        remote(gsend_b.at[lax.rem(ti + k, tiles)], grecv_b.at[ti], b_send.at[k], b_recv.at[k], tile_peer(k))
        for k in range(1, tiles)
    ]
    for y in range(quarter, 3 * quarter):
        encode(y)
    for copy in b_copies:
        copy.wait()
    total = gsum[ti]
    for k in range(1, tiles):
        total += grecv_b[lax.rem(ti + k, tiles)].astype(F32)
    grecv_c[ph] = total.astype(BF16)
    c_copies = [
        remote(grecv_c.at[ph], grecv_c.at[ph], c_send.at[k], c_recv.at[k], phase_peer(k))
        for k in range(1, phases)
    ]
    for y in range(3 * quarter, grid_rows):
        encode(y)
    for copy in c_copies:
        copy.wait()
    total = grecv_c[0].astype(F32)
    for p in range(1, phases):
        total += grecv_c[p].astype(F32)
    gfin[...] = total
    last = remote(gfin, gfin_other, d_send, d_recv, partner)
    grad_ref[dp] = total
    last.wait()
    grad_ref[other] = gfin_other[...]


def fused_body(camera_feats, backbone_w, depth_w, block_tile, point_slot, block_cells, bev_w, cotangent):
    phases, tiles = lax.axis_size("phase"), lax.axis_size("tile")
    micro, _, cams, _, width, channels = camera_feats.shape
    pos = cams * width
    groups = pos // BLK
    seg = depth_w.shape[1] // NSEG
    slots = block_cells.shape[-1]
    grid_rows, grid_cols = cotangent.shape[2:4]
    cells = grid_rows * grid_cols
    side = [(0, 0), (0, 0), (0, 128 - seg)]
    bins = NSEG * 128
    heads = jnp.pad(depth_w.reshape(channels, NSEG, seg), side).reshape(channels, bins)
    point = point_slot.reshape(groups, NSEG, BLK, seg).transpose(0, 2, 1, 3).reshape(pos, NSEG, seg)
    point = jnp.pad(point, side).reshape(pos, bins)
    local = block_cells.reshape(groups * NSEG, slots)
    code = block_tile.reshape(groups * NSEG, 1) * cells + local
    code = jnp.where(local < cells, code, 1 << 24).reshape(1, groups * NSEG * slots)
    total = micro * cotangent.shape[1] * lax.axis_size("dp") * cells * tiles
    dims = (phases, tiles, width, slots, bins, seg, grid_rows, grid_cols, float(total) ** (-0.5))
    rows = code.shape[1]
    cols = 9 * channels
    pad_pos = -(-pos // 128) * 128
    dma = pltpu.SemaphoreType.DMA
    vmem = pl.BlockSpec(memory_space=pltpu.VMEM)
    scratch = [
        pltpu.VMEM((tiles * pos, channels), BF16),
        pltpu.VMEM(((tiles + 2) * pos, 3 * channels), BF16),
        pltpu.VMEM((phases, cols, channels), BF16),
        pltpu.VMEM((1, tiles * rows), jnp.int32),
        pltpu.VMEM((pad_pos, 128), BF16),
        pltpu.VMEM((tiles, NSEG * slots, pad_pos), BF16),
        pltpu.VMEM((pad_pos, NSEG * slots), BF16),
        pltpu.VMEM((width, width // BLK * NSEG * slots), BF16),
        pltpu.VMEM((channels, cells), BF16),
        pltpu.VMEM(((grid_rows + 2) * channels, grid_cols), F32),
        pltpu.VMEM(((grid_rows + 2) * grid_cols, 3 * channels), BF16),
        pltpu.VMEM((2, tiles, 16, cols), F32),
        pltpu.VMEM((2, tiles, 16, cols), BF16),
        pltpu.VMEM((tiles, 16, cols), BF16),
        pltpu.VMEM((tiles, 16, cols), F32),
        pltpu.VMEM((tiles, 16, cols), BF16),
        pltpu.VMEM((tiles, 16, cols), BF16),
        pltpu.VMEM((phases, 16, cols), BF16),
        pltpu.VMEM((16, cols), F32),
        pltpu.VMEM((16, cols), F32),
        dma((3,)),
        dma((2, tiles, cams)), dma((tiles, cams)), dma((tiles,)), dma((tiles,)),
        dma((phases,)), dma((phases,)), dma((phases,)), dma((phases,)),
        dma((tiles,)), dma((tiles,)),
        dma(()), dma(()),
        dma((tiles,)), dma((tiles,)),
        dma((phases,)), dma((phases,)),
        dma(()), dma(()),
    ]
    encoded, grad = pl.pallas_call(
        functools.partial(fused_kernel, dims),
        out_shape=(
            jax.ShapeDtypeStruct((cells, channels), BF16),
            jax.ShapeDtypeStruct((2, 16, cols), F32),
        ),
        in_specs=[vmem] * 7,
        out_specs=(vmem, vmem),
        scratch_shapes=scratch,
        compiler_params=pltpu.CompilerParams(
            collective_id=0, has_side_effects=True, vmem_limit_bytes=48 * 1024 * 1024
        ),
        name="lift_splat",
    )(
        camera_feats.reshape(micro, pos, channels),
        backbone_w[0],
        heads,
        point,
        code,
        bev_w,
        cotangent.reshape(cells, channels),
    )
    return encoded.reshape(cotangent.shape), grad.reshape(32, cols)


def solution(mesh):
    return jax.shard_map(
        fused_body if mesh.shape["tile"] == 4 else body,
        mesh=mesh,
        in_specs=(
            P(None, "dp", None, "tile", None, None),
            P("phase", None, None),
            P(),
            P("phase", "dp", "tile", None),
            P("phase", "dp", "tile", None),
            P("phase", "dp", "tile", None),
            P(),
            P("phase", "dp", "tile", None, None),
        ),
        out_specs=(P("phase", "dp", "tile", None, None), P("tile", None)),
        check_vma=False,
    )
```
